512 devices in a mesh: rep: 8 (over y), fsdp: 64 (over z, x, core).
Axes of the slice: x: 4, y: 8, z: 8, core: 2. Of those that a mesh axis runs over, the one named last changes fastest.
Arguments:
- grad_partials: bfloat16 [8, 64, 64, 14336], P('rep', None, 'fsdp'), may hold values from -5 to 5
- stats_prev: float32 [8, 64, 1, 2, 512, 512], P('rep', 'fsdp'), may hold values from -10 to 5401, as said below
- owner_table: int32 [224], replicated, may hold values from 0 to 63, as said below
- newton_counts: int32 [224], replicated, may hold values from 2 to 3
Outputs:
- direction: bfloat16 [64, 64, 14336], P('rep', 'fsdp')
The draws below stay inside these ranges and needn't reach their ends.
Inputs may be any that keep to these rules, and one draw needn't show every extreme that they name: `owner_table`: block b belongs to replica group b // 28; within a group no two blocks have the same value; a value v names the single slot of fsdp index v. `stats_prev`: each 512 x 512 matrix is symmetric positive definite.
All inputs are finite; a program needn't handle non-finite values.
Results may differ from the reference program's by a relative error of at most 0.019.
Values may be sent and summed in bfloat16 or wider, within the bound.
A program may use at most 64 MiB of HBM per device.

```python
import jax
import jax.numpy as jnp
from jax import lax

B = 512
ROWS = 4096
COLS = 14336
NEWTON = 3
NBR = 8
NBC = 28
NBLK = 224
BPR = 1
SLOTS = 1
N_REP = 8
N_FSDP = 64


def draw_stats_prev(key, part):
    key = jax.random.fold_in(key, 11)
    first_key, second_key = jax.random.split(key)
    full_shape = (N_REP, N_FSDP, SLOTS, 2, B, B)
    uniform_raw = jax.random.uniform(first_key, full_shape, jnp.float32, -1.0, 1.0)
    symmetric = 0.5 * (uniform_raw + jnp.swapaxes(uniform_raw, -1, -2))
    identity = jnp.eye(B, dtype=jnp.float32)
    dominant = symmetric * (1.0 - identity) + 1.05 * B * identity
    spread = 3.0
    log_scales = jax.random.uniform(second_key, full_shape[:-1], jnp.float32, -1.0, 1.0) * jnp.log(spread)
    row_scale = jnp.exp(0.5 * log_scales)
    return dominant * row_scale[..., :, None] * row_scale[..., None, :]


def draw_owner_table(key, part):
    key = jax.random.fold_in(key, 23)
    places = N_FSDP * SLOTS
    per_group = BPR * NBC
    subkeys = jax.random.split(key, N_REP)

    def one_group(group_key):
        middle = jax.random.permutation(group_key, places - 2) + 1
        ends = jnp.array([places - 1, 0], dtype=middle.dtype)
        ordered = jnp.concatenate([ends, middle])
        return ordered[:per_group]
    return jax.vmap(one_group)(subkeys).reshape(NBLK).astype(jnp.int32)


def draw_newton_counts(key, part):
    key = jax.random.fold_in(key, 37)
    first_key, second_key = jax.random.split(key)
    counts = jax.random.randint(first_key, (NBLK,), 2, NEWTON + 1)
    forced_at = jax.random.randint(second_key, (), 0, NBLK)
    counts = counts.at[forced_at].set(NEWTON)
    counts = counts.at[(forced_at + 1) % NBLK].set(2)
    return counts.astype(jnp.int32)


def levels(rng, extent, cuts, low, largest):
    def one(position, blocks):
        draws = jax.random.uniform(jax.random.fold_in(jax.random.fold_in(rng, 6), position), (blocks,), jnp.float32, low / len(cuts), largest / len(cuts))
        return jnp.repeat(jnp.exp(draws), extent[position] // blocks).reshape((-1,) + (1,) * (len(extent) - position - 1))

    level = one(*cuts[0])
    for cut in cuts[1:]:
        level = level * one(*cut)
    return level


def centred(stream_key, extent, scale, reach, cuts=(), kind=jnp.bfloat16):
    values = jax.random.normal(stream_key, extent, jnp.float32) * scale
    if len(cuts) > 0:
        values = levels(stream_key, extent, cuts, -0.22, 0.18) * values
    return jnp.clip(values, min=-reach, max=reach).astype(kind)


def setup_inputs(seed: int = 0) -> dict:
    key_list = jax.random.split(jax.random.key(seed), 5)
    grad_partials = centred(key_list[0], (N_REP, ROWS // N_FSDP, N_FSDP, COLS), 0.35, 5.0, ((0, 8), (2, 64)))
    stats_prev = draw_stats_prev(jax.random.fold_in(key_list[4], 71), 0)
    owner_table = draw_owner_table(jax.random.fold_in(key_list[4], 71), 0)
    newton_counts = draw_newton_counts(jax.random.fold_in(key_list[4], 71), 0)
    return {"grad_partials": grad_partials, "stats_prev": stats_prev, "owner_table": owner_table, "newton_counts": newton_counts}


def inverse_root(statistic, iter_count):
    identity = jnp.eye(statistic.shape[0], dtype=jnp.float32)
    newton_m = statistic / jnp.sqrt(jnp.sum(statistic * statistic) + 1e-06)
    step_t = ((5.0 * identity - newton_m) * 0.25).astype(jnp.bfloat16)
    power_p = step_t.astype(jnp.float32)

    def advance(step_index, carried):
        newton_m, step_t, power_p = carried
        square_t = jnp.dot(step_t, step_t, preferred_element_type=jnp.float32).astype(jnp.bfloat16)
        fourth_t = jnp.dot(square_t, square_t, preferred_element_type=jnp.float32).astype(jnp.bfloat16)
        newton_m = jnp.dot(fourth_t, newton_m.astype(jnp.bfloat16), preferred_element_type=jnp.float32)
        step_t = ((5.0 * identity - newton_m) * 0.25).astype(jnp.bfloat16)
        power_p = jnp.dot(power_p.astype(jnp.bfloat16), step_t, preferred_element_type=jnp.float32)
        return (newton_m, step_t, power_p)
    carried = lax.fori_loop(0, iter_count - 1, advance, (newton_m, step_t, power_p))
    return carried[2].astype(jnp.bfloat16)

def reference(grad_partials, stats_prev, owner_table, newton_counts):
    summed = lax.optimization_barrier(jnp.sum(grad_partials, axis=0, dtype=jnp.float32))
    grad_matrix = summed.reshape(ROWS, COLS)
    block_grid = grad_matrix.reshape(NBR, B, NBC, B).transpose(0, 2, 1, 3).reshape(NBLK, B, B)

    def one_block(block_id):
        grad_block = block_grid[block_id]
        value = owner_table[block_id]
        group_id = block_id // (BPR * NBC)
        previous = stats_prev[group_id, value // SLOTS, value % SLOTS]
        left_stat = 0.9 * previous[0] + jnp.dot(grad_block, grad_block.T, precision=lax.Precision.HIGHEST)
        right_stat = 0.9 * previous[1] + jnp.dot(grad_block.T, grad_block, precision=lax.Precision.HIGHEST)
        iter_count = newton_counts[block_id]
        left_root = inverse_root(left_stat, iter_count)
        right_root = inverse_root(right_stat, iter_count)
        halfway = jnp.dot(left_root.astype(jnp.float32), grad_block, precision=lax.Precision.HIGHEST)
        precond = jnp.dot(halfway, right_root.astype(jnp.float32), precision=lax.Precision.HIGHEST)
        grad_mass = jnp.sum(grad_block * grad_block)
        pre_mass = jnp.sum(precond * precond)
        return (precond * jnp.sqrt(grad_mass / (pre_mass + 1e-06))).astype(jnp.bfloat16)
    results = lax.map(one_block, jnp.arange(NBLK, dtype=jnp.int32))
    return results.reshape(NBR, NBC, B, B).transpose(0, 2, 1, 3).reshape(ROWS // N_FSDP, N_FSDP, COLS)
```

```python
import functools

import jax
import jax.numpy as jnp
from jax import lax
from jax.experimental import pallas as pl
from jax.experimental.pallas import tpu as pltpu
from jax.sharding import PartitionSpec as P

F32 = jnp.float32
BF16 = jnp.bfloat16
PARTS = 2


def mm(a, b, dims=((1,), (0,))):
    return lax.dot_general(a, b, (dims, ((), ())), preferred_element_type=F32)


def kernel(
    n_rep, n_fsdp, n_col,
    x_hbm, s_hbm, owner_ref, count_ref, out_ref,
    x_v, s_v, ring_out, ring_in, summed, packed, g_in, g_f, g_n, d_f, d_out, d_in,
    blk_v, blk_s,
    x_sem, s_sem, blk_sem, ring_send, ring_recv, fwd_send, fwd_recv, back_send, back_recv,
):
    rep = lax.axis_index("rep")
    me = lax.axis_index("fsdp")
    block = s_v.shape[-1]
    width = block // PARTS
    half = n_col // 2
    far = n_rep // 2
    up = lax.rem(rep + 1, n_rep)
    down = lax.rem(rep + n_rep - 1, n_rep)

    barrier = pltpu.get_barrier_semaphore()
    for peer in (up, down):
        pl.semaphore_signal(barrier, inc=1, device_id={"rep": peer}, device_id_type=pl.DeviceIdType.MESH)

    def greet(t, carry):
        w = lax.rem(me + t, n_fsdp)
        pl.semaphore_signal(barrier, inc=1, device_id={"fsdp": w}, device_id_type=pl.DeviceIdType.MESH)
        return carry

    lax.fori_loop(1, n_fsdp, greet, 0)

    def x_copy(k):
        d = lax.rem(rep + k, n_rep)
        return pltpu.make_async_copy(x_hbm.at[d], x_v.at[d], x_sem.at[k])

    order = [far]
    for k in range(far - 1, 0, -1):
        order += [k, n_rep - k]
    order.append(0)
    for k in order:
        x_copy(k).start()
    s_copy = pltpu.make_async_copy(s_hbm, s_v, s_sem)
    s_copy.start()

    lanes = lax.broadcasted_iota(jnp.int32, blk_v.shape, 1)
    slots = jnp.zeros(blk_v.shape, jnp.int32)
    for j in range(n_col):
        slots = jnp.where(lanes == owner_ref[rep * n_col + j], j, slots)
    blk_v[...] = slots
    blk_copy = pltpu.make_async_copy(blk_v, blk_s, blk_sem)
    blk_copy.start()
    x_copy(far).wait()
    pl.semaphore_wait(barrier, n_fsdp + 1)

    def own(k, j, c):
        d = lax.rem(rep + k, n_rep)
        start = pl.multiple_of(j * block + c * width, 128)
        return x_v[d, :, pl.ds(start, width)]

    def ring_copy(way, s, c):
        lo = half * way if s == 0 else 0
        size = half if s == 0 else n_col
        return pltpu.make_async_remote_copy(
            src_ref=ring_out.at[way, s, c, pl.ds(lo, size)],
            dst_ref=ring_in.at[way, s, c, pl.ds(lo, size)],
            send_sem=ring_send.at[way, s, c],
            recv_sem=ring_recv.at[way, s, c],
            device_id={"rep": up if way == 0 else down},
            device_id_type=pl.DeviceIdType.MESH,
        )

    waited = {far}

    def ring_step(s, c):
        for way in range(2):
            k = far - s if way == 0 else n_rep - far + s
            if k not in waited:
                waited.add(k)
                x_copy(k).wait()
            if s > 0:
                ring_copy(way, s - 1, c).wait_recv()

            def add(j, carry):
                total = ring_in[way, s - 1, c, j].astype(F32) + own(k, j, c).astype(F32)
                ring_out[way, s, c, j] = total.astype(BF16)
                return carry

            def keep(j, carry):
                ring_out[way, s, c, j] = own(k, j, c)
                return carry

            lo = half * way
            other = half - lo
            if s == 0:
                lax.fori_loop(lo, lo + half, keep, 0)
            elif s == 1:
                lax.fori_loop(lo, lo + half, add, 0)
                lax.fori_loop(other, other + half, keep, 0)
            else:
                lax.fori_loop(0, n_col, add, 0)
            ring_copy(way, s, c).start()

    def fwd_copy(w, c):
        return pltpu.make_async_remote_copy(
            src_ref=packed.at[c, w],
            dst_ref=g_in.at[c, me],
            send_sem=fwd_send.at[c],
            recv_sem=fwd_recv.at[c],
            device_id={"fsdp": w},
            device_id_type=pl.DeviceIdType.MESH,
        )

    def finish(c):
        if 0 not in waited:
            waited.add(0)
            x_copy(0).wait()
        for way in range(2):
            ring_copy(way, far - 1, c).wait_recv()

        def add(j, carry):
            total = own(0, j, c).astype(F32)
            for way in range(2):
                total = total + ring_in[way, far - 1, c, j].astype(F32)
            summed[c, j] = total.astype(BF16)
            return carry

        lax.fori_loop(0, n_col, add, 0)

        def send(t, carry):
            w = lax.rem(me + t, n_fsdp)
            packed[c, w] = summed[c, blk_s[0, w]]
            fwd_copy(w, c).start()
            return carry

        lax.fori_loop(1, n_fsdp, send, 0)
        g_in[c, me] = summed[c, blk_s[0, me]]

    blk_copy.wait()
    for s in range(far):
        for c in range(PARTS):
            ring_step(s, c)
    for c in range(PARTS):
        finish(c)

    s_copy.wait()
    for c in range(PARTS):
        filled = g_in.at[c, pl.ds(0, n_fsdp - 1)]
        pltpu.make_async_copy(filled, filled, fwd_recv.at[c]).wait()
        lines = g_in[c].astype(F32).reshape(block, width)
        for q in range(width // 128):
            g_f[c * (width // 128) + q] = lines[:, q * 128:(q + 1) * 128]
    thin = block // n_fsdp
    for q in range(block // 128):
        for a in range(thin):
            g_n[a * n_fsdp:(a + 1) * n_fsdp, q * 128:(q + 1) * 128] = g_f[
                q, pl.ds(a, n_fsdp, stride=thin), :
            ].astype(BF16)

    grad = g_n[...]
    grad32 = grad.astype(F32)
    grad_mass = jnp.sum(grad32 * grad32)
    stats = [
        0.9 * s_v[0] + mm(grad, grad, ((1,), (1,))),
        0.9 * s_v[1] + mm(grad, grad, ((0,), (0,))),
    ]
    row = lax.broadcasted_iota(jnp.int32, (block, block), 0)
    col = lax.broadcasted_iota(jnp.int32, (block, block), 1)
    five = jnp.where(row == col, 1.25, 0.0)
    more = count_ref[rep * n_col + blk_s[0, me]] > 2

    newton = [a * (1.0 / jnp.sqrt(jnp.sum(a * a) + 1e-6)) for a in stats]
    step = [(five - 0.25 * m).astype(BF16) for m in newton]
    newton = [m.astype(BF16) for m in newton]
    power = list(step)
    first = None
    for it in range(2):
        square = [mm(t, t).astype(BF16) for t in step]
        fourth = [mm(t, t).astype(BF16) for t in square]
        newton32 = [mm(fourth[i], newton[i]) for i in range(2)]
        step = [(five - 0.25 * m).astype(BF16) for m in newton32]
        newton = [m.astype(BF16) for m in newton32]
        power = [mm(power[i], step[i]).astype(BF16) for i in range(2)]
        if it == 0:
            first = power
    roots = [jnp.where(more, power[i], first[i]) for i in range(2)]
    halfway = mm(roots[0], grad).astype(BF16)
    precond = mm(halfway, roots[1])
    pre_mass = jnp.sum(precond * precond)
    scaled = precond * jnp.sqrt(grad_mass / (pre_mass + 1e-6))
    for q in range(block // 128):
        d_f[q] = scaled[:, q * 128:(q + 1) * 128]

    def back_copy(w):
        return pltpu.make_async_remote_copy(
            src_ref=d_out.at[w],
            dst_ref=d_in.at[me],
            send_sem=back_send,
            recv_sem=back_recv,
            device_id={"fsdp": w},
            device_id_type=pl.DeviceIdType.MESH,
        )

    def lines_of(w):
        return jnp.concatenate(
            [d_f[q, pl.ds(w, thin, stride=n_fsdp), :] for q in range(block // 128)], axis=1
        ).astype(BF16)

    def send_back(t, carry):
        w = lax.rem(me + t, n_fsdp)
        d_out[w] = lines_of(w)
        back_copy(w).start()
        return carry

    lax.fori_loop(1, n_fsdp, send_back, 0)
    d_in[me] = lines_of(me)

    filled = d_in.at[pl.ds(0, n_fsdp - 1)]
    pltpu.make_async_copy(filled, filled, back_recv).wait()
    for j in range(n_col):
        out_ref[:, j * block:(j + 1) * block] = d_in[owner_ref[rep * n_col + j]]

    for way in range(2):
        for s in range(far):
            for c in range(PARTS):
                ring_copy(way, s, c).wait_send()
    for c in range(PARTS):
        sent = packed.at[c, pl.ds(0, n_fsdp - 1)]
        pltpu.make_async_copy(sent, sent, fwd_send.at[c]).wait()
    sent = d_out.at[pl.ds(0, n_fsdp - 1)]
    pltpu.make_async_copy(sent, sent, back_send).wait()


def body(grad_partials, stats_prev, owner_table, newton_counts):
    n_rep = lax.axis_size("rep")
    n_fsdp = lax.axis_size("fsdp")
    cols = grad_partials.shape[3]
    block = stats_prev.shape[-1]
    n_col = cols // block
    lines = grad_partials.shape[1] // n_rep
    far = n_rep // 2
    width = block // PARTS
    x = grad_partials.reshape(n_rep, lines, cols)
    s = stats_prev.reshape(2, block, block)
    out = pl.pallas_call(
        functools.partial(kernel, n_rep, n_fsdp, n_col),
        out_shape=jax.ShapeDtypeStruct((lines, cols), BF16),
        in_specs=[
            pl.BlockSpec(memory_space=pl.ANY),
            pl.BlockSpec(memory_space=pl.ANY),
            pl.BlockSpec(memory_space=pltpu.SMEM),
            pl.BlockSpec(memory_space=pltpu.SMEM),
        ],
        out_specs=pl.BlockSpec(memory_space=pltpu.VMEM),
        scratch_shapes=[
            pltpu.VMEM((n_rep, lines, cols), BF16),
            pltpu.VMEM((2, block, block), F32),
            pltpu.VMEM((2, far, PARTS, n_col, lines, width), BF16),
            pltpu.VMEM((2, far, PARTS, n_col, lines, width), BF16),
            pltpu.VMEM((PARTS, n_col, lines, width), BF16),
            pltpu.VMEM((PARTS, n_fsdp, lines, width), BF16),
            pltpu.VMEM((PARTS, n_fsdp, lines, width), BF16),
            pltpu.VMEM((block // 128, block, 128), F32),
            pltpu.VMEM((block, block), BF16),
            pltpu.VMEM((block // 128, block, 128), F32),
            pltpu.VMEM((n_fsdp, lines, block), BF16),
            pltpu.VMEM((n_fsdp, lines, block), BF16),
            pltpu.VMEM((8, 128), jnp.int32),
            pltpu.SMEM((8, 128), jnp.int32),
            pltpu.SemaphoreType.DMA((n_rep,)),
            pltpu.SemaphoreType.DMA,
            pltpu.SemaphoreType.DMA,
            pltpu.SemaphoreType.DMA((2, far, PARTS)),
            pltpu.SemaphoreType.DMA((2, far, PARTS)),
            pltpu.SemaphoreType.DMA((PARTS,)),
            pltpu.SemaphoreType.DMA((PARTS,)),
            pltpu.SemaphoreType.DMA,
            pltpu.SemaphoreType.DMA,
        ],
        compiler_params=pltpu.CompilerParams(
            collective_id=0, has_side_effects=True, vmem_limit_bytes=48 * 1024 * 1024
        ),
        cost_estimate=pl.CostEstimate(
            flops=40 * block**3, bytes_accessed=6 * 1024 * 1024, transcendentals=0
        ),
    )(x, s, owner_table, newton_counts)
    return out.reshape(lines, 1, cols)


def solution(mesh):
    return jax.shard_map(
        body,
        mesh=mesh,
        in_specs=(P("rep", None, "fsdp", None), P("rep", "fsdp", None, None, None, None), P(), P()),
        out_specs=P("rep", "fsdp", None),
        check_vma=False,
    )
```

```python
import functools

import jax
import jax.numpy as jnp
from jax import lax
from jax.experimental import pallas as pl
from jax.experimental.pallas import tpu as pltpu
from jax.sharding import PartitionSpec as P

F32 = jnp.float32
BF16 = jnp.bfloat16
PARTS = 2
INNER = 8
DEPTH = 2
GROUP = 14


def mm(a, b, dims=((1,), (0,))):
    return lax.dot_general(a, b, (dims, ((), ())), preferred_element_type=F32)


def kernel(
    n_rep, n_fsdp, n_col,
    x_hbm, s_hbm, owner_ref, count_ref, out_ref,
    x_v, s_v, ring_out, ring_in, summed, packed, g_in, g_f, g_n, d_f, d_out, d_in,
    blk_v, blk_s,
    x_sem, s_sem, blk_sem, ring_send, ring_recv, fwd_send, fwd_recv, back_send, back_recv, near_sem,
):
    rep = lax.axis_index("rep")
    me = lax.axis_index("fsdp")
    outer = n_fsdp // INNER
    plane = me // INNER
    place = lax.rem(me, INNER)
    block = s_v.shape[-1]
    width = block // PARTS
    groups = n_col // GROUP
    far = n_rep // 2
    thin = block // n_fsdp
    up = lax.rem(rep + 1, n_rep)
    down = lax.rem(rep + n_rep - 1, n_rep)

    barrier = pltpu.get_barrier_semaphore()

    def greet(sem, **peer):
        pl.semaphore_signal(sem, inc=1, device_id=peer, device_id_type=pl.DeviceIdType.MESH)

    def greet_planes(t, carry):
        greet(barrier, fsdp=lax.rem(plane + t, outer) * INNER + place)
        return carry

    def greet_places(t, carry):
        greet(barrier, fsdp=plane * INNER + lax.rem(place + t, INNER))
        return carry

    def greet_near(t, carry):
        greet(near_sem, fsdp=plane * INNER + lax.rem(place + t, INNER))
        return carry

    def x_copy(k):
        d = lax.rem(rep + k, n_rep)
        return pltpu.make_async_copy(x_hbm.at[d], x_v.at[d], x_sem.at[k])

    order = [far]
    for k in range(far - 1, 0, -1):
        order += [k, n_rep - k]
    order.append(0)

    x_copy(far).start()
    greet(barrier, rep=up)
    greet(barrier, rep=down)
    lax.fori_loop(1, outer, greet_planes, 0)
    lax.fori_loop(1, INNER, greet_places, 0)
    for k in order[1:]:
        x_copy(k).start()
    s_copy = pltpu.make_async_copy(s_hbm, s_v, s_sem)
    s_copy.start()

    lanes = lax.broadcasted_iota(jnp.int32, blk_v.shape, 1)
    slots = jnp.zeros(blk_v.shape, jnp.int32)
    for j in range(n_col):
        slots = jnp.where(lanes == owner_ref[rep * n_col + j], j, slots)
    blk_v[...] = slots
    blk_copy = pltpu.make_async_copy(blk_v, blk_s, blk_sem)
    blk_copy.start()

    def own(k, j, p):
        d = lax.rem(rep + k, n_rep)
        return x_v[d, :, j * block + p * width:j * block + (p + 1) * width]

    def ring_copy(way, s, p, g):
        return pltpu.make_async_remote_copy(
            src_ref=ring_out.at[way, s, p, pl.ds(g * GROUP, GROUP)],
            dst_ref=ring_in.at[way, s, p, pl.ds(g * GROUP, GROUP)],
            send_sem=ring_send.at[way, s, p, g],
            recv_sem=ring_recv.at[way, s, p, g],
            device_id={"rep": up if way == 0 else down},
            device_id_type=pl.DeviceIdType.MESH,
        )

    waited = set()

    def x_wait(k):
        if k not in waited:
            waited.add(k)
            x_copy(k).wait()

    def starts(way, g):
        return (g < groups // 2) == (way == 0)

    flight = ([], [])

    def ring_step(way, s, p, g):
        k = far - s if way == 0 else n_rep - far + s
        x_wait(k)
        joined = s > 1 or (s == 1 and starts(way, g))
        if joined:
            ring_copy(way, s - 1, p, g).wait_recv()
        for j in range(g * GROUP, (g + 1) * GROUP):
            mine = own(k, j, p)
            ring_out[way, s, p, j] = ring_in[way, s - 1, p, j] + mine if joined else mine
        if len(flight[way]) == DEPTH:
            flight[way].pop(0).wait_send()
        flight[way].append(ring_copy(way, s, p, g))
        flight[way][-1].start()

    def finish(p, g):
        x_wait(0)
        for way in range(2):
            ring_copy(way, far - 1, p, g).wait_recv()
        for j in range(g * GROUP, (g + 1) * GROUP):
            total = own(0, j, p).astype(F32)
            for way in range(2):
                total = total + ring_in[way, far - 1, p, j].astype(F32)
            summed[p, j] = total.astype(BF16)

    def fwd_copy(w, p):
        return pltpu.make_async_remote_copy(
            src_ref=packed.at[p, w],
            dst_ref=g_in.at[p, me],
            send_sem=fwd_send.at[p],
            recv_sem=fwd_recv.at[p],
            device_id={"fsdp": w},
            device_id_type=pl.DeviceIdType.MESH,
        )

    def forward(p, lo, hi):
        def send(t, carry):
            w = lax.rem(me + t, n_fsdp)
            packed[p, w] = summed[p, blk_s[0, w]]
            fwd_copy(w, p).start()
            return carry

        lax.fori_loop(lo, hi, send, 0)

    def await_bytes(sem, buffer):
        part = buffer.at[pl.ds(0, n_fsdp - 1)]
        pltpu.make_async_copy(part, part, sem).wait()

    def gather(p):
        g_in[p, me] = summed[p, blk_s[0, me]]
        await_bytes(fwd_recv.at[p], g_in.at[p])
        lines = g_in[p].astype(F32).reshape(block, width)
        for q in range(width // 128):
            at = p * (width // 128) + q
            g_f[at] = lines[:, q * 128:(q + 1) * 128]
            for a in range(thin):
                g_n[p, a * n_fsdp:(a + 1) * n_fsdp, q * 128:(q + 1) * 128] = g_f[
                    at, pl.ds(a, n_fsdp, stride=thin), :
                ].astype(BF16)

    def drain():
        for way in range(2):
            for copy in flight[way]:
                copy.wait_send()
        for p in range(PARTS):
            await_bytes(fwd_send.at[p], packed.at[p])
        await_bytes(back_send, d_out)

    x_wait(far)
    blk_copy.wait()
    pl.semaphore_wait(barrier, outer + INNER)

    def pairs(p, s, kind):
        first = [[g for g in range(groups) if starts(way, g)] for way in range(2)]
        rest = [[g for g in range(groups) if not starts(way, g)] for way in range(2)]
        picked = [{"first": first, "rest": rest, "all": [rest[i] + first[i] for i in range(2)]}[kind][i] for i in range(2)]
        return [[(0, s, p, g), (1, s, p, h)] for g, h in zip(*picked)]

    def steps(p):
        return [pairs(p, 0, "first"), pairs(p, 1, "rest"), pairs(p, 1, "first")] + [
            pairs(p, s, "all") for s in range(2, far)
        ]

    def run(list_of_pairs):
        for pair in list_of_pairs:
            for step in pair:
                ring_step(*step)

    part0, part1 = steps(0), steps(1)
    run(part0[0])
    lax.fori_loop(1, INNER, greet_near, 0)
    run(part1[0])
    for a, b in zip(part0[1:], part1[1:]):
        run(a)
        run(b)
    pl.semaphore_wait(near_sem, INNER - 1)
    for p in range(PARTS):
        for g in range(groups):
            finish(p, g)
        forward(p, 1, n_fsdp)
    s_copy.wait()
    gather(0)
    left = g_n[0]
    grad32 = left.astype(F32)
    grad_mass = jnp.sum(grad32 * grad32)
    s_v[0] = 0.9 * s_v[0] + mm(left, left, ((1,), (1,)))
    s_v[1] = 0.9 * s_v[1]
    s_v[1, :width, :width] = s_v[1, :width, :width] + mm(left, left, ((0,), (0,)))
    gather(1)
    right = g_n[1]
    grad32 = right.astype(F32)
    grad_mass = grad_mass + jnp.sum(grad32 * grad32)
    across = mm(left, right, ((0,), (0,)))
    stats = [
        s_v[0] + mm(right, right, ((1,), (1,))),
        s_v[1] + jnp.concatenate(
            [
                jnp.concatenate([jnp.zeros((width, width), F32), across], axis=1),
                jnp.concatenate([mm(right, left, ((0,), (0,))), mm(right, right, ((0,), (0,)))], axis=1),
            ],
            axis=0,
        ),
    ]
    grad = jnp.concatenate([left, right], axis=1)
    row = lax.broadcasted_iota(jnp.int32, (block, block), 0)
    col = lax.broadcasted_iota(jnp.int32, (block, block), 1)
    five = jnp.where(row == col, 1.25, 0.0)
    more = count_ref[rep * n_col + blk_s[0, me]] > 2

    newton = [a * (1.0 / jnp.sqrt(jnp.sum(a * a) + 1e-6)) for a in stats]
    step = [(five - 0.25 * m).astype(BF16) for m in newton]
    newton = [m.astype(BF16) for m in newton]
    power = list(step)
    first = None
    for it in range(2):
        square = [mm(t, t).astype(BF16) for t in step]
        fourth = [mm(t, t).astype(BF16) for t in square]
        newton32 = [mm(fourth[i], newton[i]) for i in range(2)]
        step = [(five - 0.25 * m).astype(BF16) for m in newton32]
        newton = [m.astype(BF16) for m in newton32]
        power = [mm(power[i], step[i]).astype(BF16) for i in range(2)]
        if it == 0:
            first = power
    roots = [jnp.where(more, power[i], first[i]) for i in range(2)]
    halfway = mm(roots[0], grad).astype(BF16)
    precond = mm(halfway, roots[1])
    pre_mass = jnp.sum(precond * precond)
    scaled = precond * jnp.sqrt(grad_mass / (pre_mass + 1e-6))
    for q in range(block // 128):
        d_f[q] = scaled[:, q * 128:(q + 1) * 128]

    def back_copy(w):
        return pltpu.make_async_remote_copy(
            src_ref=d_out.at[w],
            dst_ref=d_in.at[me],
            send_sem=back_send,
            recv_sem=back_recv,
            device_id={"fsdp": w},
            device_id_type=pl.DeviceIdType.MESH,
        )

    def lines_of(w):
        return jnp.concatenate(
            [d_f[q, pl.ds(w, thin, stride=n_fsdp), :] for q in range(block // 128)], axis=1
        ).astype(BF16)

    def send_back(t, carry):
        w = lax.rem(me + t, n_fsdp)
        d_out[w] = lines_of(w)
        back_copy(w).start()
        return carry

    def send_both(i, carry):
        send_back(n_fsdp // 2 - i, carry)
        return send_back(n_fsdp // 2 + i, carry)

    send_back(n_fsdp // 2, 0)
    lax.fori_loop(1, n_fsdp // 2, send_both, 0)
    d_in[me] = lines_of(me)

    await_bytes(back_recv, d_in)
    for j in range(n_col):
        out_ref[:, j * block:(j + 1) * block] = d_in[owner_ref[rep * n_col + j]]

    drain()


def body(grad_partials, stats_prev, owner_table, newton_counts):
    n_rep = lax.axis_size("rep")
    n_fsdp = lax.axis_size("fsdp")
    cols = grad_partials.shape[3]
    block = stats_prev.shape[-1]
    n_col = cols // block
    lines = grad_partials.shape[1] // n_rep
    far = n_rep // 2
    width = block // PARTS
    x = grad_partials.reshape(n_rep, lines, cols)
    s = stats_prev.reshape(2, block, block)
    out = pl.pallas_call(
        functools.partial(kernel, n_rep, n_fsdp, n_col),
        out_shape=jax.ShapeDtypeStruct((lines, cols), BF16),
        in_specs=[
            pl.BlockSpec(memory_space=pl.ANY),
            pl.BlockSpec(memory_space=pl.ANY),
            pl.BlockSpec(memory_space=pltpu.SMEM),
            pl.BlockSpec(memory_space=pltpu.SMEM),
        ],
        out_specs=pl.BlockSpec(memory_space=pltpu.VMEM),
        scratch_shapes=[
            pltpu.VMEM((n_rep, lines, cols), BF16),
            pltpu.VMEM((2, block, block), F32),
            pltpu.VMEM((2, far, PARTS, n_col, lines, width), BF16),
            pltpu.VMEM((2, far, PARTS, n_col, lines, width), BF16),
            pltpu.VMEM((PARTS, n_col, lines, width), BF16),
            pltpu.VMEM((PARTS, n_fsdp, lines, width), BF16),
            pltpu.VMEM((PARTS, n_fsdp, lines, width), BF16),
            pltpu.VMEM((block // 128, block, 128), F32),
            pltpu.VMEM((PARTS, block, width), BF16),
            pltpu.VMEM((block // 128, block, 128), F32),
            pltpu.VMEM((n_fsdp, lines, block), BF16),
            pltpu.VMEM((n_fsdp, lines, block), BF16),
            pltpu.VMEM((8, 128), jnp.int32),
            pltpu.SMEM((8, 128), jnp.int32),
            pltpu.SemaphoreType.DMA((n_rep,)),
            pltpu.SemaphoreType.DMA,
            pltpu.SemaphoreType.DMA,
            pltpu.SemaphoreType.DMA((2, far, PARTS, n_col // GROUP)),
            pltpu.SemaphoreType.DMA((2, far, PARTS, n_col // GROUP)),
            pltpu.SemaphoreType.DMA((PARTS,)),
            pltpu.SemaphoreType.DMA((PARTS,)),
            pltpu.SemaphoreType.DMA,
            pltpu.SemaphoreType.DMA,
            pltpu.SemaphoreType.REGULAR,
        ],
        compiler_params=pltpu.CompilerParams(
            collective_id=0, has_side_effects=True, vmem_limit_bytes=60 * 1024 * 1024
        ),
        cost_estimate=pl.CostEstimate(
            flops=40 * block**3, bytes_accessed=6 * 1024 * 1024, transcendentals=0
        ),
    )(x, s, owner_table, newton_counts)
    return out.reshape(lines, 1, cols)


def solution(mesh):
    return jax.shard_map(
        body,
        mesh=mesh,
        in_specs=(P("rep", None, "fsdp", None), P("rep", "fsdp", None, None, None, None), P(), P()),
        out_specs=P("rep", "fsdp", None),
        check_vma=False,
    )
```

```python
import functools

import jax
import jax.numpy as jnp
from jax import lax
from jax.experimental import pallas as pl
from jax.experimental.pallas import tpu as pltpu
from jax.sharding import PartitionSpec as P

F32 = jnp.float32
BF16 = jnp.bfloat16
PARTS = 2
INNER = 8
DEPTH = 2
GROUP = 14


def mm(a, b, dims=((1,), (0,))):
    return lax.dot_general(a, b, (dims, ((), ())), preferred_element_type=F32)


def kernel(
    n_rep, n_fsdp, n_col,
    x_hbm, s_hbm, owner_hbm, count_hbm, out_ref,
    x_v, s_v, ring_out, ring_in, summed, packed, g_in, packed0, mid0, g_in0, g_f, g_n, d_f, d_out, d_in,
    owner_ref, count_ref, blk_v, blk_s,
    x_sem, s_sem, table_sem, blk_sem, ring_send, ring_recv, fwd_send, fwd_recv, back_send, back_recv, near_sem, mid_send, mid_recv,
):
    rep = lax.axis_index("rep")
    me = lax.axis_index("fsdp")
    outer = n_fsdp // INNER
    plane = me // INNER
    place = lax.rem(me, INNER)
    block = s_v.shape[-1]
    width = block // PARTS
    groups = n_col // GROUP
    far = n_rep // 2
    thin = block // n_fsdp
    up = lax.rem(rep + 1, n_rep)
    down = lax.rem(rep + n_rep - 1, n_rep)

    barrier = pltpu.get_barrier_semaphore()

    def greet(sem, **peer):
        pl.semaphore_signal(sem, inc=1, device_id=peer, device_id_type=pl.DeviceIdType.MESH)

    def greet_planes(t, carry):
        greet(barrier, fsdp=lax.rem(plane + t, outer) * INNER + place)
        return carry

    def greet_places(t, carry):
        greet(barrier, fsdp=plane * INNER + lax.rem(place + t, INNER))
        return carry

    def greet_near(t, carry):
        greet(near_sem, fsdp=plane * INNER + lax.rem(place + t, INNER))
        return carry

    def x_copy(k):
        d = lax.rem(rep + k, n_rep)
        return pltpu.make_async_copy(x_hbm.at[d], x_v.at[d], x_sem.at[k])

    order = [far]
    for k in range(far - 1, 0, -1):
        order += [k, n_rep - k]
    order.append(0)

    x_copy(far).start()
    tables = [
        pltpu.make_async_copy(owner_hbm, owner_ref, table_sem.at[0]),
        pltpu.make_async_copy(count_hbm, count_ref, table_sem.at[1]),
    ]
    for copy in tables:
        copy.start()
    greet(barrier, rep=up)
    greet(barrier, rep=down)
    lax.fori_loop(1, outer, greet_planes, 0)
    lax.fori_loop(1, INNER, greet_places, 0)
    for k in order[1:]:
        x_copy(k).start()
    s_copy = pltpu.make_async_copy(s_hbm, s_v, s_sem)
    s_copy.start()

    for copy in tables:
        copy.wait()
    lanes = lax.broadcasted_iota(jnp.int32, blk_v.shape, 1)
    slots = jnp.zeros(blk_v.shape, jnp.int32)
    for j in range(n_col):
        slots = jnp.where(lanes == owner_ref[rep * n_col + j], j, slots)
    blk_v[...] = slots
    blk_copy = pltpu.make_async_copy(blk_v, blk_s, blk_sem)
    blk_copy.start()

    def own(k, j, p):
        d = lax.rem(rep + k, n_rep)
        return x_v[d, :, j * block + p * width:j * block + (p + 1) * width]

    def ring_copy(way, s, p, g):
        return pltpu.make_async_remote_copy(
            src_ref=ring_out.at[way, s, p, pl.ds(g * GROUP, GROUP)],
            dst_ref=ring_in.at[way, s, p, pl.ds(g * GROUP, GROUP)],
            send_sem=ring_send.at[way, s, p, g],
            recv_sem=ring_recv.at[way, s, p, g],
            device_id={"rep": up if way == 0 else down},
            device_id_type=pl.DeviceIdType.MESH,
        )

    waited = set()

    def x_wait(k):
        if k not in waited:
            waited.add(k)
            x_copy(k).wait()

    def starts(way, g):
        return (g < groups // 2) == (way == 0)

    flight = ([], [])

    def ring_step(way, s, p, g):
        k = far - s if way == 0 else n_rep - far + s
        x_wait(k)
        joined = s > 1 or (s == 1 and starts(way, g))
        if joined:
            ring_copy(way, s - 1, p, g).wait_recv()
        for j in range(g * GROUP, (g + 1) * GROUP):
            mine = own(k, j, p)
            ring_out[way, s, p, j] = ring_in[way, s - 1, p, j] + mine if joined else mine
        if len(flight[way]) == DEPTH:
            flight[way].pop(0).wait_send()
        flight[way].append(ring_copy(way, s, p, g))
        flight[way][-1].start()

    def finish(p, g):
        x_wait(0)
        for way in range(2):
            ring_copy(way, far - 1, p, g).wait_recv()
        for j in range(g * GROUP, (g + 1) * GROUP):
            total = own(0, j, p).astype(F32)
            for way in range(2):
                total = total + ring_in[way, far - 1, p, j].astype(F32)
            summed[p, j] = total.astype(BF16)

    def plane_copy(t):
        z = lax.rem(plane + t, outer)
        return pltpu.make_async_remote_copy(
            src_ref=packed0.at[z],
            dst_ref=mid0.at[plane],
            send_sem=mid_send,
            recv_sem=mid_recv,
            device_id={"fsdp": z * INNER + place},
            device_id_type=pl.DeviceIdType.MESH,
        )

    def place_copy(t):
        u = lax.rem(place + t, INNER)
        return pltpu.make_async_remote_copy(
            src_ref=mid0.at[:, u],
            dst_ref=g_in0.at[:, place],
            send_sem=fwd_send.at[0],
            recv_sem=fwd_recv.at[0],
            device_id={"fsdp": plane * INNER + u},
            device_id_type=pl.DeviceIdType.MESH,
        )

    def to_planes():
        def send(t, carry):
            z = lax.rem(plane + t, outer)
            for u in range(INNER):
                packed0[z, u] = summed[0, blk_s[0, z * INNER + u]]
            plane_copy(t).start()
            return carry

        lax.fori_loop(1, outer, send, 0)
        for u in range(INNER):
            mid0[plane, u] = summed[0, blk_s[0, plane * INNER + u]]

    def to_places():
        await_bytes(mid_recv, mid0, outer)

        def send(t, carry):
            place_copy(t).start()
            return carry

        lax.fori_loop(1, INNER, send, 0)
        for z in range(outer):
            g_in0[z, place] = mid0[z, place]

    def fwd_copy(w):
        return pltpu.make_async_remote_copy(
            src_ref=packed.at[w],
            dst_ref=g_in.at[me],
            send_sem=fwd_send.at[1],
            recv_sem=fwd_recv.at[1],
            device_id={"fsdp": w},
            device_id_type=pl.DeviceIdType.MESH,
        )

    def forward(lo, hi):
        def send(t, carry):
            w = lax.rem(me + t, n_fsdp)
            packed[w] = summed[1, blk_s[0, w]]
            fwd_copy(w).start()
            return carry

        lax.fori_loop(lo, hi, send, 0)

    def await_bytes(sem, buffer, count):
        part = buffer.at[pl.ds(0, count - 1)]
        pltpu.make_async_copy(part, part, sem).wait()

    def gather(p):
        if p == 0:
            await_bytes(fwd_recv.at[0], g_in0, INNER)
            lines = g_in0[...].astype(F32).reshape(block, width)
        else:
            g_in[me] = summed[1, blk_s[0, me]]
            await_bytes(fwd_recv.at[1], g_in, n_fsdp)
            lines = g_in[...].astype(F32).reshape(block, width)
        for q in range(width // 128):
            at = p * (width // 128) + q
            g_f[at] = lines[:, q * 128:(q + 1) * 128]
            for a in range(thin):
                g_n[p, a * n_fsdp:(a + 1) * n_fsdp, q * 128:(q + 1) * 128] = g_f[
                    at, pl.ds(a, n_fsdp, stride=thin), :
                ].astype(BF16)

    def drain():
        for way in range(2):
            for copy in flight[way]:
                copy.wait_send()
        await_bytes(mid_send, packed0, outer)
        await_bytes(fwd_send.at[0], mid0, INNER)
        await_bytes(fwd_send.at[1], packed, n_fsdp)
        await_bytes(back_send, d_out, n_fsdp)

    x_wait(far)
    blk_copy.wait()
    pl.semaphore_wait(barrier, outer + INNER)

    def pairs(p, s, kind):
        first = [[g for g in range(groups) if starts(way, g)] for way in range(2)]
        rest = [[g for g in range(groups) if not starts(way, g)] for way in range(2)]
        picked = [{"first": first, "rest": rest, "all": [rest[i] + first[i] for i in range(2)]}[kind][i] for i in range(2)]
        return [[(0, s, p, g), (1, s, p, h)] for g, h in zip(*picked)]

    def steps(p):
        return [pairs(p, 0, "first"), pairs(p, 1, "rest"), pairs(p, 1, "first")] + [
            pairs(p, s, "all") for s in range(2, far)
        ]

    def run(list_of_pairs):
        for pair in list_of_pairs:
            for step in pair:
                ring_step(*step)

    part0, part1 = steps(0), steps(1)
    run(part0[0])
    lax.fori_loop(1, INNER, greet_near, 0)
    for stage in (part0[1], part0[2], part1[0], part1[1], part0[3], part1[2], part0[4], part1[3]):
        run(stage)
    for g in range(groups):
        finish(0, g)
    to_planes()
    for stage in (part1[4],):
        run(stage)
    pl.semaphore_wait(near_sem, INNER - 1)
    for g in range(groups):
        finish(1, g)
    forward(1, n_fsdp)
    to_places()
    s_copy.wait()
    gather(0)
    left = g_n[0]
    grad32 = left.astype(F32)
    grad_mass = jnp.sum(grad32 * grad32)
    s_v[0] = 0.9 * s_v[0] + mm(left, left, ((1,), (1,)))
    s_v[1] = 0.9 * s_v[1]
    s_v[1, :width, :width] = s_v[1, :width, :width] + mm(left, left, ((0,), (0,)))
    gather(1)
    right = g_n[1]
    grad32 = right.astype(F32)
    grad_mass = grad_mass + jnp.sum(grad32 * grad32)
    across = mm(left, right, ((0,), (0,)))
    stats = [
        s_v[0] + mm(right, right, ((1,), (1,))),
        s_v[1] + jnp.concatenate(
            [
                jnp.concatenate([jnp.zeros((width, width), F32), across], axis=1),
                jnp.concatenate([mm(right, left, ((0,), (0,))), mm(right, right, ((0,), (0,)))], axis=1),
            ],
            axis=0,
        ),
    ]
    grad = jnp.concatenate([left, right], axis=1)
    row = lax.broadcasted_iota(jnp.int32, (block, block), 0)
    col = lax.broadcasted_iota(jnp.int32, (block, block), 1)
    five = jnp.where(row == col, 1.25, 0.0)
    more = count_ref[rep * n_col + blk_s[0, me]] > 2

    newton = [a * (1.0 / jnp.sqrt(jnp.sum(a * a) + 1e-6)) for a in stats]
    step = [(five - 0.25 * m).astype(BF16) for m in newton]
    newton = [m.astype(BF16) for m in newton]
    power = list(step)
    first = None
    for it in range(2):
        square = [mm(t, t).astype(BF16) for t in step]
        fourth = [mm(t, t).astype(BF16) for t in square]
        newton32 = [mm(fourth[i], newton[i]) for i in range(2)]
        step = [(five - 0.25 * m).astype(BF16) for m in newton32]
        newton = [m.astype(BF16) for m in newton32]
        power = [mm(power[i], step[i]).astype(BF16) for i in range(2)]
        if it == 0:
            first = power
    roots = [jnp.where(more, power[i], first[i]) for i in range(2)]
    halfway = mm(roots[0], grad).astype(BF16)
    precond = mm(halfway, roots[1])
    pre_mass = jnp.sum(precond * precond)
    scaled = precond * jnp.sqrt(grad_mass / (pre_mass + 1e-6))
    for q in range(block // 128):
        d_f[q] = scaled[:, q * 128:(q + 1) * 128]

    def back_copy(w):
        return pltpu.make_async_remote_copy(
            src_ref=d_out.at[w],
            dst_ref=d_in.at[me],
            send_sem=back_send,
            recv_sem=back_recv,
            device_id={"fsdp": w},
            device_id_type=pl.DeviceIdType.MESH,
        )

    def lines_of(w):
        return jnp.concatenate(
            [d_f[q, pl.ds(w, thin, stride=n_fsdp), :] for q in range(block // 128)], axis=1
        ).astype(BF16)

    def send_back(t, carry):
        w = lax.rem(me + t, n_fsdp)
        d_out[w] = lines_of(w)
        back_copy(w).start()
        return carry

    def send_both(i, carry):
        send_back(n_fsdp // 2 - i, carry)
        return send_back(n_fsdp // 2 + i, carry)

    send_back(n_fsdp // 2, 0)
    lax.fori_loop(1, n_fsdp // 2, send_both, 0)
    d_in[me] = lines_of(me)

    await_bytes(back_recv, d_in, n_fsdp)
    for j in range(n_col):
        out_ref[:, j * block:(j + 1) * block] = d_in[owner_ref[rep * n_col + j]]

    drain()


def body(grad_partials, stats_prev, owner_table, newton_counts):
    n_rep = lax.axis_size("rep")
    n_fsdp = lax.axis_size("fsdp")
    cols = grad_partials.shape[3]
    block = stats_prev.shape[-1]
    n_col = cols // block
    lines = grad_partials.shape[1] // n_rep
    far = n_rep // 2
    width = block // PARTS
    x = grad_partials.reshape(n_rep, lines, cols)
    s = stats_prev.reshape(2, block, block)
    out = pl.pallas_call(
        functools.partial(kernel, n_rep, n_fsdp, n_col),
        out_shape=jax.ShapeDtypeStruct((lines, cols), BF16),
        in_specs=[
            pl.BlockSpec(memory_space=pltpu.HBM),
            pl.BlockSpec(memory_space=pltpu.HBM),
            pl.BlockSpec(memory_space=pltpu.HBM),
            pl.BlockSpec(memory_space=pltpu.HBM),
        ],
        out_specs=pl.BlockSpec(memory_space=pltpu.VMEM),
        scratch_shapes=[
            pltpu.VMEM((n_rep, lines, cols), BF16),
            pltpu.VMEM((2, block, block), F32),
            pltpu.VMEM((2, far, PARTS, n_col, lines, width), BF16),
            pltpu.VMEM((2, far, PARTS, n_col, lines, width), BF16),
            pltpu.VMEM((PARTS, n_col, lines, width), BF16),
            pltpu.VMEM((n_fsdp, lines, width), BF16),
            pltpu.VMEM((n_fsdp, lines, width), BF16),
            pltpu.VMEM((n_fsdp // INNER, INNER, lines, width), BF16),
            pltpu.VMEM((n_fsdp // INNER, INNER, lines, width), BF16),
            pltpu.VMEM((n_fsdp // INNER, INNER, lines, width), BF16),
            pltpu.VMEM((block // 128, block, 128), F32),
            pltpu.VMEM((PARTS, block, width), BF16),
            pltpu.VMEM((block // 128, block, 128), F32),
            pltpu.VMEM((n_fsdp, lines, block), BF16),
            pltpu.VMEM((n_fsdp, lines, block), BF16),
            pltpu.SMEM(owner_table.shape, jnp.int32),
            pltpu.SMEM(newton_counts.shape, jnp.int32),
            pltpu.VMEM((8, 128), jnp.int32),
            pltpu.SMEM((8, 128), jnp.int32),
            pltpu.SemaphoreType.DMA((n_rep,)),
            pltpu.SemaphoreType.DMA,
            pltpu.SemaphoreType.DMA((2,)),
            pltpu.SemaphoreType.DMA,
            pltpu.SemaphoreType.DMA((2, far, PARTS, n_col // GROUP)),
            pltpu.SemaphoreType.DMA((2, far, PARTS, n_col // GROUP)),
            pltpu.SemaphoreType.DMA((PARTS,)),
            pltpu.SemaphoreType.DMA((PARTS,)),
            pltpu.SemaphoreType.DMA,
            pltpu.SemaphoreType.DMA,
            pltpu.SemaphoreType.REGULAR,
            pltpu.SemaphoreType.DMA,
            pltpu.SemaphoreType.DMA,
        ],
        compiler_params=pltpu.CompilerParams(
            collective_id=0, has_side_effects=True, vmem_limit_bytes=40 * 1024 * 1024
        ),
        cost_estimate=pl.CostEstimate(
            flops=40 * block**3, bytes_accessed=6 * 1024 * 1024, transcendentals=0
        ),
    )(*[pltpu.with_memory_space_constraint(v, pltpu.HBM) for v in (x, s, owner_table, newton_counts)])
    return out.reshape(lines, 1, cols)


def solution(mesh):
    return jax.shard_map(
        body,
        mesh=mesh,
        in_specs=(P("rep", None, "fsdp", None), P("rep", "fsdp", None, None, None, None), P(), P()),
        out_specs=P("rep", "fsdp", None),
        check_vma=False,
    )
```

```python
import functools

import jax
import jax.numpy as jnp
from jax import lax
from jax.experimental import pallas as pl
from jax.experimental.pallas import tpu as pltpu
from jax.sharding import PartitionSpec as P

F32 = jnp.float32
BF16 = jnp.bfloat16
PARTS = 2
INNER = 8
DEPTH = 4
GROUP = 7


def mm(a, b, dims=((1,), (0,))):
    return lax.dot_general(a, b, (dims, ((), ())), preferred_element_type=F32)


def kernel(
    n_rep, n_fsdp, n_col,
    x_hbm, s_hbm, owner_hbm, count_hbm, out_ref,
    x_v, s_v, ring_out, ring_in, summed, packed, g_in, packed0, mid0, g_in0, g_f, g_n, d_f, d_out, d_in,
    owner_ref, count_ref, blk_v, blk_s,
    x_sem, s_sem, table_sem, blk_sem, ring_send, ring_recv, fwd_send, fwd_recv, back_send, back_recv, near_sem, mid_send, mid_recv,
):
    rep = lax.axis_index("rep")
    me = lax.axis_index("fsdp")
    outer = n_fsdp // INNER
    plane = me // INNER
    place = lax.rem(me, INNER)
    block = s_v.shape[-1]
    width = block // PARTS
    groups = n_col // GROUP
    far = n_rep // 2
    thin = block // n_fsdp
    up = lax.rem(rep + 1, n_rep)
    down = lax.rem(rep + n_rep - 1, n_rep)

    barrier = pltpu.get_barrier_semaphore()

    def greet(sem, **peer):
        pl.semaphore_signal(sem, inc=1, device_id=peer, device_id_type=pl.DeviceIdType.MESH)

    def greet_planes(t, carry):
        greet(barrier, fsdp=lax.rem(plane + t, outer) * INNER + place)
        return carry

    def greet_places(t, carry):
        greet(barrier, fsdp=plane * INNER + lax.rem(place + t, INNER))
        return carry

    def greet_near(t, carry):
        greet(near_sem, fsdp=plane * INNER + lax.rem(place + t, INNER))
        return carry

    def x_copy(k):
        d = lax.rem(rep + k, n_rep)
        return pltpu.make_async_copy(x_hbm.at[d], x_v.at[d], x_sem.at[k])

    order = [far]
    for k in range(far - 1, 0, -1):
        order += [k, n_rep - k]
    order.append(0)

    x_copy(far).start()
    tables = [
        pltpu.make_async_copy(owner_hbm, owner_ref, table_sem.at[0]),
        pltpu.make_async_copy(count_hbm, count_ref, table_sem.at[1]),
    ]
    for copy in tables:
        copy.start()
    greet(barrier, rep=up)
    greet(barrier, rep=down)
    lax.fori_loop(1, outer, greet_planes, 0)
    lax.fori_loop(1, INNER, greet_places, 0)
    for k in order[1:]:
        x_copy(k).start()
    s_copy = pltpu.make_async_copy(s_hbm, s_v, s_sem)
    s_copy.start()

    for copy in tables:
        copy.wait()
    lanes = lax.broadcasted_iota(jnp.int32, blk_v.shape, 1)
    slots = jnp.zeros(blk_v.shape, jnp.int32)
    for j in range(n_col):
        slots = jnp.where(lanes == owner_ref[rep * n_col + j], j, slots)
    blk_v[...] = slots
    blk_copy = pltpu.make_async_copy(blk_v, blk_s, blk_sem)
    blk_copy.start()

    def own(k, j, p):
        d = lax.rem(rep + k, n_rep)
        return x_v[d, :, j * block + p * width:j * block + (p + 1) * width]

    def ring_copy(way, s, p, g):
        return pltpu.make_async_remote_copy(
            src_ref=ring_out.at[way, s, p, pl.ds(g * GROUP, GROUP)],
            dst_ref=ring_in.at[way, s, p, pl.ds(g * GROUP, GROUP)],
            send_sem=ring_send.at[way, s, p, g],
            recv_sem=ring_recv.at[way, s, p, g],
            device_id={"rep": up if way == 0 else down},
            device_id_type=pl.DeviceIdType.MESH,
        )

    waited = set()

    def x_wait(k):
        if k not in waited:
            waited.add(k)
            x_copy(k).wait()

    def starts(way, g):
        return (g < groups // 2) == (way == 0)

    flight = ([], [])

    def ring_step(way, s, p, g):
        k = far - s if way == 0 else n_rep - far + s
        x_wait(k)
        joined = s > 1 or (s == 1 and starts(way, g))
        if joined:
            ring_copy(way, s - 1, p, g).wait_recv()
        for j in range(g * GROUP, (g + 1) * GROUP):
            mine = own(k, j, p)
            ring_out[way, s, p, j] = ring_in[way, s - 1, p, j] + mine if joined else mine
        if len(flight[way]) == DEPTH:
            flight[way].pop(0).wait_send()
        flight[way].append(ring_copy(way, s, p, g))
        flight[way][-1].start()

    def finish(p, g):
        x_wait(0)
        for way in range(2):
            ring_copy(way, far - 1, p, g).wait_recv()
        for j in range(g * GROUP, (g + 1) * GROUP):
            total = own(0, j, p).astype(F32)
            for way in range(2):
                total = total + ring_in[way, far - 1, p, j].astype(F32)
            summed[p, j] = total.astype(BF16)

    def plane_copy(t):
        z = lax.rem(plane + t, outer)
        return pltpu.make_async_remote_copy(
            src_ref=packed0.at[z],
            dst_ref=mid0.at[plane],
            send_sem=mid_send,
            recv_sem=mid_recv,
            device_id={"fsdp": z * INNER + place},
            device_id_type=pl.DeviceIdType.MESH,
        )

    def place_copy(t):
        u = lax.rem(place + t, INNER)
        return pltpu.make_async_remote_copy(
            src_ref=mid0.at[:, u],
            dst_ref=g_in0.at[:, place],
            send_sem=fwd_send.at[0],
            recv_sem=fwd_recv.at[0],
            device_id={"fsdp": plane * INNER + u},
            device_id_type=pl.DeviceIdType.MESH,
        )

    def to_planes():
        def send(t, carry):
            z = lax.rem(plane + t, outer)
            for u in range(INNER):
                packed0[z, u] = summed[0, blk_s[0, z * INNER + u]]
            plane_copy(t).start()
            return carry

        lax.fori_loop(1, outer, send, 0)
        for u in range(INNER):
            mid0[plane, u] = summed[0, blk_s[0, plane * INNER + u]]

    def to_places():
        await_bytes(mid_recv, mid0, outer)

        def send(t, carry):
            place_copy(t).start()
            return carry

        lax.fori_loop(1, INNER, send, 0)
        for z in range(outer):
            g_in0[z, place] = mid0[z, place]

    def fwd_copy(w):
        return pltpu.make_async_remote_copy(
            src_ref=packed.at[w],
            dst_ref=g_in.at[me],
            send_sem=fwd_send.at[1],
            recv_sem=fwd_recv.at[1],
            device_id={"fsdp": w},
            device_id_type=pl.DeviceIdType.MESH,
        )

    def forward(lo, hi):
        def send(t, carry):
            w = lax.rem(me + t, n_fsdp)
            packed[w] = summed[1, blk_s[0, w]]
            fwd_copy(w).start()
            return carry

        lax.fori_loop(lo, hi, send, 0)

    def await_bytes(sem, buffer, count):
        part = buffer.at[pl.ds(0, count - 1)]
        pltpu.make_async_copy(part, part, sem).wait()

    def gather(p):
        if p == 0:
            await_bytes(fwd_recv.at[0], g_in0, INNER)
            lines = g_in0[...].astype(F32).reshape(block, width)
        else:
            g_in[me] = summed[1, blk_s[0, me]]
            await_bytes(fwd_recv.at[1], g_in, n_fsdp)
            lines = g_in[...].astype(F32).reshape(block, width)
        for q in range(width // 128):
            at = p * (width // 128) + q
            g_f[at] = lines[:, q * 128:(q + 1) * 128]
            for a in range(thin):
                g_n[p, a * n_fsdp:(a + 1) * n_fsdp, q * 128:(q + 1) * 128] = g_f[
                    at, pl.ds(a, n_fsdp, stride=thin), :
                ].astype(BF16)

    def drain():
        for way in range(2):
            for copy in flight[way]:
                copy.wait_send()
        await_bytes(mid_send, packed0, outer)
        await_bytes(fwd_send.at[0], mid0, INNER)
        await_bytes(fwd_send.at[1], packed, n_fsdp)
        await_bytes(back_send, d_out, n_fsdp)

    x_wait(far)
    blk_copy.wait()
    pl.semaphore_wait(barrier, outer + INNER)

    def pairs(p, s, kind):
        first = [[g for g in range(groups) if starts(way, g)] for way in range(2)]
        rest = [[g for g in range(groups) if not starts(way, g)] for way in range(2)]
        picked = [{"first": first, "rest": rest, "all": [rest[i] + first[i] for i in range(2)]}[kind][i] for i in range(2)]
        return [[(0, s, p, g), (1, s, p, h)] for g, h in zip(*picked)]

    def steps(p):
        return [pairs(p, 0, "first"), pairs(p, 1, "rest"), pairs(p, 1, "first")] + [
            pairs(p, s, "all") for s in range(2, far)
        ]

    def run(list_of_pairs):
        for pair in list_of_pairs:
            for step in pair:
                ring_step(*step)

    part0, part1 = steps(0), steps(1)
    run(part0[0])
    lax.fori_loop(1, INNER, greet_near, 0)
    for stage in (part0[1], part0[2], part1[0], part1[1], part0[3], part1[2], part0[4], part1[3]):
        run(stage)
    for g in range(groups):
        finish(0, g)
    to_planes()
    for stage in (part1[4],):
        run(stage)
    pl.semaphore_wait(near_sem, INNER - 1)
    for g in range(groups):
        finish(1, g)
    forward(1, n_fsdp)
    to_places()
    s_copy.wait()
    gather(0)
    left = g_n[0]
    grad32 = left.astype(F32)
    grad_mass = jnp.sum(grad32 * grad32)
    s_v[0] = 0.9 * s_v[0] + mm(left, left, ((1,), (1,)))
    s_v[1] = 0.9 * s_v[1]
    s_v[1, :width, :width] = s_v[1, :width, :width] + mm(left, left, ((0,), (0,)))
    gather(1)
    right = g_n[1]
    grad32 = right.astype(F32)
    grad_mass = grad_mass + jnp.sum(grad32 * grad32)
    across = mm(left, right, ((0,), (0,)))
    stats = [
        s_v[0] + mm(right, right, ((1,), (1,))),
        s_v[1] + jnp.concatenate(
            [
                jnp.concatenate([jnp.zeros((width, width), F32), across], axis=1),
                jnp.concatenate([mm(right, left, ((0,), (0,))), mm(right, right, ((0,), (0,)))], axis=1),
            ],
            axis=0,
        ),
    ]
    grad = jnp.concatenate([left, right], axis=1)
    row = lax.broadcasted_iota(jnp.int32, (block, block), 0)
    col = lax.broadcasted_iota(jnp.int32, (block, block), 1)
    five = jnp.where(row == col, 1.25, 0.0)
    more = count_ref[rep * n_col + blk_s[0, me]] > 2

    newton = [a * (1.0 / jnp.sqrt(jnp.sum(a * a) + 1e-6)) for a in stats]
    step = [(five - 0.25 * m).astype(BF16) for m in newton]
    newton = [m.astype(BF16) for m in newton]
    power = list(step)
    first = None
    for it in range(2):
        square = [mm(t, t).astype(BF16) for t in step]
        fourth = [mm(t, t).astype(BF16) for t in square]
        newton32 = [mm(fourth[i], newton[i]) for i in range(2)]
        step = [(five - 0.25 * m).astype(BF16) for m in newton32]
        newton = [m.astype(BF16) for m in newton32]
        power = [mm(power[i], step[i]).astype(BF16) for i in range(2)]
        if it == 0:
            first = power
    roots = [jnp.where(more, power[i], first[i]) for i in range(2)]
    halfway = mm(roots[0], grad).astype(BF16)
    precond = mm(halfway, roots[1])
    pre_mass = jnp.sum(precond * precond)
    scale = jnp.sqrt(grad_mass / (pre_mass + 1e-6))
    for q in range(block // 128):
        d_f[q] = precond[:, q * 128:(q + 1) * 128]

    def back_copy(w):
        return pltpu.make_async_remote_copy(
            src_ref=d_out.at[w],
            dst_ref=d_in.at[me],
            send_sem=back_send,
            recv_sem=back_recv,
            device_id={"fsdp": w},
            device_id_type=pl.DeviceIdType.MESH,
        )

    def lines_of(w):
        lines = [d_f[q, pl.ds(w, thin, stride=n_fsdp), :] for q in range(block // 128)]
        return (jnp.concatenate(lines, axis=1) * scale).astype(BF16)

    def send_back(t, carry):
        w = lax.rem(me + t, n_fsdp)
        d_out[w] = lines_of(w)
        back_copy(w).start()
        return carry

    def send_both(i, carry):
        send_back(n_fsdp // 2 - i, carry)
        return send_back(n_fsdp // 2 + i, carry)

    send_back(n_fsdp // 2, 0)
    lax.fori_loop(1, n_fsdp // 2, send_both, 0)
    d_in[me] = lines_of(me)

    await_bytes(back_recv, d_in, n_fsdp)
    for j in range(n_col):
        out_ref[:, j * block:(j + 1) * block] = d_in[owner_ref[rep * n_col + j]]

    drain()


def body(grad_partials, stats_prev, owner_table, newton_counts):
    n_rep = lax.axis_size("rep")
    n_fsdp = lax.axis_size("fsdp")
    cols = grad_partials.shape[3]
    block = stats_prev.shape[-1]
    n_col = cols // block
    lines = grad_partials.shape[1] // n_rep
    far = n_rep // 2
    width = block // PARTS
    x = grad_partials.reshape(n_rep, lines, cols)
    s = stats_prev.reshape(2, block, block)
    out = pl.pallas_call(
        functools.partial(kernel, n_rep, n_fsdp, n_col),
        out_shape=jax.ShapeDtypeStruct((lines, cols), BF16),
        in_specs=[
            pl.BlockSpec(memory_space=pltpu.HBM),
            pl.BlockSpec(memory_space=pltpu.HBM),
            pl.BlockSpec(memory_space=pltpu.HBM),
            pl.BlockSpec(memory_space=pltpu.HBM),
        ],
        out_specs=pl.BlockSpec(memory_space=pltpu.VMEM),
        scratch_shapes=[
            pltpu.VMEM((n_rep, lines, cols), BF16),
            pltpu.VMEM((2, block, block), F32),
            pltpu.VMEM((2, far, PARTS, n_col, lines, width), BF16),
            pltpu.VMEM((2, far, PARTS, n_col, lines, width), BF16),
            pltpu.VMEM((PARTS, n_col, lines, width), BF16),
            pltpu.VMEM((n_fsdp, lines, width), BF16),
            pltpu.VMEM((n_fsdp, lines, width), BF16),
            pltpu.VMEM((n_fsdp // INNER, INNER, lines, width), BF16),
            pltpu.VMEM((n_fsdp // INNER, INNER, lines, width), BF16),
            pltpu.VMEM((n_fsdp // INNER, INNER, lines, width), BF16),
            pltpu.VMEM((block // 128, block, 128), F32),
            pltpu.VMEM((PARTS, block, width), BF16),
            pltpu.VMEM((block // 128, block, 128), F32),
            pltpu.VMEM((n_fsdp, lines, block), BF16),
            pltpu.VMEM((n_fsdp, lines, block), BF16),
            pltpu.SMEM(owner_table.shape, jnp.int32),
            pltpu.SMEM(newton_counts.shape, jnp.int32),
            pltpu.VMEM((8, 128), jnp.int32),
            pltpu.SMEM((8, 128), jnp.int32),
            pltpu.SemaphoreType.DMA((n_rep,)),
            pltpu.SemaphoreType.DMA,
            pltpu.SemaphoreType.DMA((2,)),
            pltpu.SemaphoreType.DMA,
            pltpu.SemaphoreType.DMA((2, far, PARTS, n_col // GROUP)),
            pltpu.SemaphoreType.DMA((2, far, PARTS, n_col // GROUP)),
            pltpu.SemaphoreType.DMA((PARTS,)),
            pltpu.SemaphoreType.DMA((PARTS,)),
            pltpu.SemaphoreType.DMA,
            pltpu.SemaphoreType.DMA,
            pltpu.SemaphoreType.REGULAR,
            pltpu.SemaphoreType.DMA,
            pltpu.SemaphoreType.DMA,
        ],
        compiler_params=pltpu.CompilerParams(
            collective_id=0, has_side_effects=True, vmem_limit_bytes=40 * 1024 * 1024
        ),
        cost_estimate=pl.CostEstimate(
            flops=40 * block**3, bytes_accessed=6 * 1024 * 1024, transcendentals=0
        ),
    )(*[pltpu.with_memory_space_constraint(v, pltpu.HBM) for v in (x, s, owner_table, newton_counts)])
    return out.reshape(lines, 1, cols)


def solution(mesh):
    return jax.shard_map(
        body,
        mesh=mesh,
        in_specs=(P("rep", None, "fsdp", None), P("rep", "fsdp", None, None, None, None), P(), P()),
        out_specs=P("rep", "fsdp", None),
        check_vma=False,
    )
```
